256 devices in a mesh: blk: 32 (over x, z), uly: 4 (over y_hi, core), rep: 2 (over y_lo).
Axes of the slice: x: 4, y: 4 (y_hi: 2, y_lo: 2; y = y_hi * 2 + y_lo), z: 8, core: 2. Of those that a mesh axis runs over, the one named last changes fastest.
Arguments:
- queries: bfloat16 [2048, 3072], P(('rep', 'blk', 'uly')), parts along dimension 0, may hold values from -8 to 8
- keys_new: bfloat16 [2048, 3072], P(('rep', 'blk', 'uly')), parts along dimension 0, may hold values from -12 to 12
- values_new: bfloat16 [2048, 3072], P(('rep', 'blk', 'uly')), parts along dimension 0, may hold values from -6 to 6
- keys_cache: bfloat16 [14336, 3072], P(('rep', 'blk'), 'uly'), parts along dimension 0, may hold values from -12 to 12
- values_cache: bfloat16 [14336, 3072], P(('rep', 'blk'), 'uly'), parts along dimension 0, may hold values from -6 to 6
- query_frame: int32 [2048], P('rep'), parts along dimension 0, may hold values from 0 to 31, never falling along the last dimension, each value on 1 to 64 neighbouring positions
- context_frame: int32 [14336], P('rep'), parts along dimension 0, may hold values from 0 to 31, never falling along the last dimension, each value on 1 to 448 neighbouring positions
Outputs:
- attended: bfloat16 [2048, 3072], P(('rep', 'blk', 'uly')), parts along dimension 0
The draws below stay inside these ranges and needn't reach their ends.
There are 2 independent parts, one for each index of `rep`. The reference program is written for one: setup_inputs(seed, part) draws one part's arguments, and reference() takes and returns one part's arrays. A program takes and returns all parts, laid end to end along the dimension named above; each array names one. Nothing has to cross between parts.
Inputs may be any that keep to these rules, and one draw needn't show every extreme that they name: `query_frame`: frame ids never fall along the group and every frame occurs. `context_frame`: frame ids never fall along the context and every frame occurs.
All inputs are finite; a program needn't handle non-finite values.
Results may differ from the reference program's by a relative error of at most 0.017.
Values may be sent and summed in bfloat16 or wider, within the bound.
A program may use at most 128 MiB of HBM per device.

```python
import math
import jax
import jax.numpy as jnp
import numpy as np
from jax import lax

H = 24
HD = 128
FRAMES = 32
QTOK = 1024
CTX = 7168


def draw_queries(key, part):
    key = jax.random.fold_in(key, 11)
    drawn = jnp.clip(1.5 * jax.random.normal(key, (QTOK, H * HD), jnp.float32), -8.0, 8.0)
    return drawn.astype(jnp.bfloat16)


def draw_keys_cache(key, part):
    key = jax.random.fold_in(key, 23)
    first_key = jax.random.fold_in(key, 0)
    drawn = jnp.clip(2.0 * jax.random.normal(first_key, (CTX, H * HD), jnp.float32), -12.0, 12.0)
    return drawn.astype(jnp.bfloat16)


def level_of(rng, extent, shards, low, top_value):
    level, own = 1.0, jax.random.fold_in(rng, 6)
    for dim, parts in shards:
        draws = jnp.exp(jax.random.uniform(jax.random.fold_in(own, dim), (parts,), jnp.float32, low / len(shards), top_value / len(shards)))
        level = level * jnp.repeat(draws, extent[dim] // parts).reshape([-1 if axis == dim else 1 for axis in range(len(extent))])
    return level


def split_up(amount, total, limit, skew):
    weights = [(1 << 20) // math.isqrt(grade ** skew) + 1 for grade in range(2, amount + 1)]
    rest, holding = total - limit - (amount - 1), [1] * (amount - 1)
    while rest > 0:
        movable = [i for i in range(amount - 1) if holding[i] < limit]
        pool, budget = sum([weights[i] for i in movable]), rest
        for i in movable:
            extra = min(limit - holding[i], max(1, budget * weights[i] // pool), rest)
            holding[i] = holding[i] + extra
            rest = rest - extra
    return np.array([limit] + holding)


def uneven(stream_key, number_of, total, bound, skew):
    if number_of == 2:
        one = jax.random.randint(stream_key, (), max(1, total - bound), min(bound, total - 1) + 1)
        return jnp.stack([one, total - one])
    tallies = jnp.asarray(split_up(number_of, total, bound, skew), jnp.int32)
    couples = (number_of - 1) // 2
    giver, taker = tallies[1:1 + 2 * couples:2], tallies[2:2 + 2 * couples:2]
    margin = jnp.minimum(giver - 1, bound - taker)
    moved = jax.random.randint(jax.random.fold_in(stream_key, 1), (couples,), 0, 1 << 20) % (margin + 1)
    tallies = tallies.at[1:1 + 2 * couples:2].set(giver - moved).at[2:2 + 2 * couples:2].set(taker + moved)
    return tallies[jax.random.permutation(jax.random.fold_in(stream_key, 2), number_of)]


def scatter_about(stream_key, shape, width, reach, cuts=(), dtype=jnp.bfloat16):
    values = jax.random.normal(stream_key, shape, jnp.float32) * width
    if len(cuts) > 0:
        values = level_of(stream_key, shape, cuts, -0.22, 0.18) * values
    return jnp.clip(values, min=-reach, max=reach).astype(dtype)


def setup_inputs(seed: int = 0, part: int = 0) -> dict:
    keys = jax.random.split(jax.random.key(seed), 8)
    part_splits = jax.random.split(jax.random.fold_in(keys[7], part), 8)
    queries = draw_queries(jax.random.fold_in(jax.random.fold_in(keys[7], part), 71), part)
    keys_new = scatter_about(part_splits[1], (QTOK, H * HD), 2.0, 12.0, ((0, 128),))
    values_new = scatter_about(part_splits[2], (QTOK, H * HD), 1.0, 6.0, ((0, 128),))
    keys_cache = draw_keys_cache(jax.random.fold_in(jax.random.fold_in(keys[7], part), 71), part)
    values_cache = scatter_about(part_splits[4], (CTX, H * HD), 1.0, 6.0, ((0, 32), (1, 4)))
    query_frame = jnp.searchsorted(jnp.cumsum(uneven(part_splits[5], FRAMES, QTOK, 2 * QTOK // FRAMES, 0)), jnp.arange(QTOK), side="right").astype(jnp.int32)
    context_frame = jnp.searchsorted(jnp.cumsum(uneven(part_splits[6], FRAMES, CTX, 2 * CTX // FRAMES, 0)), jnp.arange(CTX), side="right").astype(jnp.int32)
    return dict(queries=queries, keys_new=keys_new, values_new=values_new, keys_cache=keys_cache, values_cache=values_cache, query_frame=query_frame, context_frame=context_frame)


def reference(queries, keys_new, values_new, keys_cache, values_cache, query_frame, context_frame):
    score_scale = HD ** -0.5
    all_keys = jnp.concatenate([keys_cache, keys_new], 0)
    all_values = jnp.concatenate([values_cache, values_new], 0)
    key_frame = jnp.concatenate([context_frame, query_frame], 0)
    visible = key_frame[None, :] <= query_frame[:, None]
    head_queries = queries.reshape(QTOK, H, HD).transpose(1, 0, 2)
    head_keys = all_keys.reshape(-1, H, HD).transpose(1, 0, 2)
    head_values = all_values.reshape(-1, H, HD).transpose(1, 0, 2)

    def one_head(operands):
        query_part, key_part, value_part = operands
        scores = jnp.dot(query_part, key_part.T, preferred_element_type=jnp.float32) * score_scale
        scores = jnp.where(visible, scores, jnp.float32(-1e30))
        highest = jnp.max(scores, axis=1, keepdims=True)
        weights = jnp.where(visible, jnp.exp(scores - highest), jnp.float32(0.0))
        denominator = jnp.sum(weights, axis=1, keepdims=True)
        mixed_sum = jnp.dot(weights.astype(jnp.bfloat16), value_part, preferred_element_type=jnp.float32)
        return (mixed_sum / denominator).astype(jnp.bfloat16)

    result = lax.map(one_head, (head_queries, head_keys, head_values))
    return result.transpose(1, 0, 2).reshape(QTOK, H * HD)
```

```python
import functools
import math

import jax
import jax.numpy as jnp
from jax import lax
from jax.experimental import pallas as pl
from jax.experimental.pallas import tpu as pltpu
from jax.sharding import PartitionSpec as P

HD = 128
NX, NZ, NU = 4, 8, 4
TOK = 8
CTXB = 224
NEWB = NU * TOK
KB = CTXB + NEWB
HEADS = 6
SCALE = math.log2(math.e) / math.sqrt(HD)
LOW = -1e30
MESH = pl.DeviceIdType.MESH
F32, BF16 = jnp.float32, jnp.bfloat16


def pair_start(x):
    return 3 * (x // 2) + lax.rem(x, 2)


def kernel(
    q_ref, kn_ref, vn_ref, kc_ref, vc_ref, qf_ref, cf_ref, out_ref,
    qland, nland, vland, qall, kbuf, vbuf, kt, vt, kft, qfr, osend, orecv, fsend, frecv,
    qs, qr, ns, nr, vs, vr, zs, zr, ks, kr, os, orr, fs, fr,
):
    blk, u = lax.axis_index("blk"), lax.axis_index("uly")
    x, z = blk // NZ, lax.rem(blk, NZ)
    me = x * NU + u
    slot_a = lax.rem(x, 2)
    slot_b = 1 - slot_a
    lane_a = pl.multiple_of(slot_a * HD, HD)
    lane_b = pl.multiple_of(slot_b * HD, HD)
    partner = NX - 1 - x

    def at(x_, z_, u_):
        return {"blk": x_ * NZ + z_, "uly": u_}

    def plane(i):
        dx, du = i // NU, i % NU
        return lax.rem(x + dx, NX), lax.rem(u + du, NU)

    def along(k):
        return at(x, lax.rem(z + NZ - k, NZ), u)

    barrier = pltpu.get_barrier_semaphore()
    for i in range(1, NX * NU):
        px, pu = plane(i)
        pl.semaphore_signal(barrier, inc=1, device_id=at(px, z, pu), device_id_type=MESH)
    for k in range(1, NZ):
        pl.semaphore_signal(barrier, inc=1, device_id=along(k), device_id_type=MESH)
    pl.semaphore_wait(barrier, NX * NU - 1 + NZ - 1)

    def columns(px, pu):
        return pl.ds(pl.multiple_of((HEADS * pu + pair_start(px)) * HD, HD), 2 * HD)

    def small(src, dst, ssem, rsem):
        copies = []
        for i in range(1, NX * NU):
            px, pu = plane(i)
            copies.append(
                pltpu.make_async_remote_copy(
                    src_ref=src.at[:, columns(px, pu)],
                    dst_ref=dst.at[me],
                    send_sem=ssem.at[i],
                    recv_sem=rsem.at[me],
                    device_id=at(px, z, pu),
                    device_id_type=MESH,
                )
            )
            copies[-1].start()
        pltpu.make_async_copy(src.at[:, columns(x, u)], dst.at[me], rsem.at[me]).start()
        return copies

    def landed(dst, rsem):
        for i in range(NX * NU):
            pltpu.make_async_copy(dst.at[i], dst.at[i], rsem.at[i]).wait()

    sends = small(q_ref, qland, qs, qr)

    def cache_cols(px, slot):
        return pl.ds(pl.multiple_of((pair_start(px) + slot) * HD, HD), HD)

    def cached(i, ref, buf, px, slot, dst, local):
        rows = buf.at[dst, pl.ds(0, CTXB)]
        src = ref.at[:, cache_cols(px, slot)]
        if local:
            pltpu.make_async_copy(src, rows, kr.at[i, dst]).start()
            return
        copy = pltpu.make_async_remote_copy(
            src_ref=src,
            dst_ref=rows,
            send_sem=ks.at[i, dst] if isinstance(dst, int) else ks.at[i, px],
            recv_sem=kr.at[i, dst],
            device_id=at(px, z, u),
            device_id_type=MESH,
        )
        copy.start()
        sends.append(copy)

    for i, (ref, buf) in enumerate(((kc_ref, kbuf), (vc_ref, vbuf))):
        cached(i, ref, buf, x, slot_b, 4, True)
        cached(i, ref, buf, partner, 1 - lax.rem(partner, 2), 5, False)
    for step in (2, 1, 3):
        px = lax.rem(x + step, NX)
        for i, (ref, buf) in enumerate(((kc_ref, kbuf), (vc_ref, vbuf))):
            cached(i, ref, buf, px, lax.rem(px, 2), x, False)
    for i, (ref, buf) in enumerate(((kc_ref, kbuf), (vc_ref, vbuf))):
        cached(i, ref, buf, x, slot_a, x, True)

    sends += small(kn_ref, nland, ns, nr)
    sends += small(vn_ref, vland, vs, vr)

    lane = lax.broadcasted_iota(jnp.int32, (1, 128), 1)
    for zz in range(NZ):
        row = jnp.zeros((1, 128), jnp.int32)
        for xx in range(NX):
            part = qf_ref[pl.ds(2 * xx + zz // 4, 1), :]
            part = pltpu.roll(part, (xx * 32 - (zz % 4) * 32) % 128, 1)
            row = jnp.where(lane // 32 == xx, part, row)
        qfr[zz] = jnp.broadcast_to(row, (8, 128))
    for xx in range(NX):
        place = (xx * NZ + z) * CTXB
        first, off = place // 128, lax.rem(place, 128)
        rows = [
            pltpu.roll(
                jnp.broadcast_to(cf_ref[pl.ds(jnp.minimum(first + j, 55), 1), :], (8, 128)),
                lax.rem(128 - off, 128),
                1,
            )
            for j in range(3)
        ]
        lanes8 = lax.broadcasted_iota(jnp.int32, (8, 128), 1)
        low = jnp.where(lanes8 < 128 - off, rows[0], rows[1])
        high = jnp.where(lanes8 < 128 - off, rows[1], rows[2])
        token = (xx * NZ + z) * NEWB
        new = jnp.broadcast_to(qf_ref[pl.ds(token // 128, 1), :], (8, 128))
        new = pltpu.roll(new, lax.rem(96 + 128 - lax.rem(token, 128), 128), 1)
        high = jnp.where(lanes8 >= 96, new, high)
        for h, part in enumerate((low, high)):
            wide = jnp.broadcast_to(part[:1].astype(F32), (128, 128))
            kft[xx, pl.ds(h * 128, 128), :] = wide.T.astype(jnp.int32)

    landed(qland, qr)
    for k in range(1, NZ):
        copy = pltpu.make_async_remote_copy(
            src_ref=qland,
            dst_ref=qall.at[k],
            send_sem=zs.at[k],
            recv_sem=zr.at[k],
            device_id=at(x, lax.rem(z + k, NZ), u),
            device_id_type=MESH,
        )
        copy.start()
        sends.append(copy)
    qall[0] = qland[...]

    landed(nland, nr)
    landed(vland, vr)

    def cache_landed(dst):
        for i, buf in enumerate((kbuf, vbuf)):
            rows = buf.at[dst, pl.ds(0, CTXB)]
            pltpu.make_async_copy(rows, rows, kr.at[i, dst]).wait()

    def join(dst, xx, lanes):
        for land, buf in ((nland, kbuf), (vland, vbuf)):
            new = land[pl.ds(xx * NU, NU), :, pl.ds(lanes, HD)]
            new = new.astype(F32).reshape(NEWB, HD).astype(BF16)
            buf[dst, pl.ds(CTXB, NEWB), :] = new
        vt[dst] = vbuf[dst].T

    def order(i):
        odd = lax.rem(i, 2)
        return odd * ((i + 1) // 2) + (1 - odd) * lax.rem(NZ - i // 2, NZ)

    def attend(head, blocks, lanes, i, wait):
        k = order(i)
        if wait:

            @pl.when(k > 0)
            def _():
                pltpu.make_async_copy(qall.at[k], qall.at[k], zr.at[k]).wait()

        zz = lax.rem(z + NZ - k, NZ)
        query = qall[k, :, :, pl.ds(lanes, HD)].astype(F32).reshape(NX * NU * TOK, HD)
        query = query.astype(BF16)
        frames = qfr[zz][:1]
        scores = []
        for dst, xx in blocks:
            s = lax.dot_general(
                kbuf[dst], query, (((1,), (1,)), ((), ())), preferred_element_type=F32
            )
            scores.append(jnp.where(kft[xx] <= frames, s * SCALE, LOW))
        top = functools.reduce(jnp.maximum, [jnp.max(s, axis=0, keepdims=True) for s in scores])
        total = jnp.zeros_like(top)
        summed = jnp.zeros((HD, 128), F32)
        for (dst, _), s in zip(blocks, scores):
            w = jnp.exp2(s - top)
            total += jnp.sum(w, axis=0, keepdims=True)
            summed += jnp.dot(vt[dst], w.astype(BF16), preferred_element_type=F32)
        osend[head, k, pl.ds(0, HD), :] = (summed / total).astype(BF16)
        level = top + jnp.log2(total)
        one = level.astype(BF16).astype(F32)
        two = (level - one).astype(BF16).astype(F32)
        three = level - one - two
        row = lax.broadcasted_iota(jnp.int32, (16, 128), 0)
        rows = jnp.where(row == 0, one, jnp.where(row == 1, two, jnp.where(row == 2, three, 0.0)))
        osend[head, k, pl.ds(HD, 16), :] = rows.astype(BF16)

        @pl.when(k > 0)
        def _():
            pltpu.make_async_remote_copy(
                src_ref=osend.at[head, k],
                dst_ref=orecv.at[head, k],
                send_sem=os.at[head, k],
                recv_sem=orr.at[head, k],
                device_id=along(k),
                device_id_type=MESH,
            ).start()

    cache_landed(4)
    cache_landed(5)
    join(4, x, lane_b)
    join(5, partner, lane_b)

    def shared(i, carry):
        attend(1, ((4, x), (5, partner)), lane_b, i, True)
        return carry

    lax.fori_loop(0, NZ, shared, 0)

    for xx in range(NX):
        cache_landed(xx)
        join(xx, xx, lane_a)

    def whole(i, carry):
        attend(0, tuple((xx, xx) for xx in range(NX)), lane_a, i, False)
        return carry

    lax.fori_loop(0, NZ, whole, 0)

    def merge(head):
        for k in range(1, NZ):
            pltpu.make_async_copy(orecv.at[head, k], orecv.at[head, k], orr.at[head, k]).wait()
        parts = [osend.at[head, 0]] + [orecv.at[head, k] for k in range(1, NZ)]
        levels = []
        for part in parts:
            tail = part[pl.ds(HD, 16), :].astype(F32)
            levels.append(tail[0:1] + tail[1:2] + tail[2:3])
        top = functools.reduce(jnp.maximum, levels)
        weights = [jnp.exp2(level - top) for level in levels]
        total = functools.reduce(jnp.add, weights)
        merged = jnp.zeros((HD, 128), F32)
        for part, w in zip(parts, weights):
            merged += part[pl.ds(0, HD), :].astype(F32) * w
        return merged / total, top + jnp.log2(total)

    merged, level = merge(1)
    fsend[:, pl.ds(TOK, TOK), :] = merged.T.reshape(NX * NU, TOK, HD)
    fsend[:, pl.ds(2 * TOK, TOK), :] = jnp.broadcast_to(level, (128, 128)).T.reshape(
        NX * NU, TOK, HD
    )
    merged, _ = merge(0)
    fsend[:, pl.ds(0, TOK), :] = merged.T.reshape(NX * NU, TOK, HD)

    for i in range(1, NX * NU):
        px, pu = plane(i)
        copy = pltpu.make_async_remote_copy(
            src_ref=fsend.at[px * NU + pu],
            dst_ref=frecv.at[me],
            send_sem=fs.at[i],
            recv_sem=fr.at[me],
            device_id=at(px, z, pu),
            device_id_type=MESH,
        )
        copy.start()
        sends.append(copy)
    pltpu.make_async_copy(fsend.at[me], frecv.at[me], fr.at[me]).start()
    landed(frecv, fr)
    for uu in range(NU):
        for half in range(2):
            ends = (frecv.at[2 * half * NU + uu], frecv.at[(2 * half + 1) * NU + uu])
            base = (HEADS * uu + 3 * half) * HD
            for e, end in enumerate(ends):
                out_ref[:, pl.ds(base + 2 * e * HD, HD)] = end[pl.ds(0, TOK), :].astype(BF16)
            levels = [end[pl.ds(2 * TOK, TOK), :] for end in ends]
            top = jnp.maximum(levels[0], levels[1])
            w = [jnp.exp2(level - top) for level in levels]
            both = [end[pl.ds(TOK, TOK), :] for end in ends]
            mixed = (both[0] * w[0] + both[1] * w[1]) / (w[0] + w[1])
            out_ref[:, pl.ds(base + HD, HD)] = mixed.astype(BF16)

    for copy in sends:
        copy.wait_send()
    for head in range(2):
        for k in range(1, NZ):
            pltpu.make_async_copy(osend.at[head, k], osend.at[head, k], os.at[head, k]).wait()


def shards(queries, keys_new, values_new, keys_cache, values_cache, query_frame, context_frame):
    anywhere = pl.BlockSpec(memory_space=pl.ANY)
    vmem = pl.BlockSpec(memory_space=pltpu.VMEM)
    dma = pltpu.SemaphoreType.DMA
    n = NX * NU
    return pl.pallas_call(
        kernel,
        out_shape=jax.ShapeDtypeStruct((TOK, queries.shape[1]), BF16),
        in_specs=[anywhere] * 5 + [vmem] * 2,
        out_specs=vmem,
        scratch_shapes=[
            pltpu.VMEM((n, TOK, 2 * HD), BF16),
            pltpu.VMEM((n, TOK, 2 * HD), BF16),
            pltpu.VMEM((n, TOK, 2 * HD), BF16),
            pltpu.VMEM((NZ, n, TOK, 2 * HD), BF16),
            pltpu.VMEM((6, KB, HD), BF16),
            pltpu.VMEM((6, KB, HD), BF16),
            pltpu.VMEM((1, 16, HD), BF16),
            pltpu.VMEM((6, HD, KB), BF16),
            pltpu.VMEM((NX, KB, 128), jnp.int32),
            pltpu.VMEM((NZ, 8, 128), jnp.int32),
            pltpu.VMEM((2, NZ, HD + 16, 128), BF16),
            pltpu.VMEM((2, NZ, HD + 16, 128), BF16),
            pltpu.VMEM((n, 3 * TOK, HD), F32),
            pltpu.VMEM((n, 3 * TOK, HD), F32),
            dma((n,)), dma((n,)), dma((n,)), dma((n,)), dma((n,)), dma((n,)),
            dma((NZ,)), dma((NZ,)),
            dma((2, 6)), dma((2, 6)),
            dma((2, NZ)), dma((2, NZ)),
            dma((n,)), dma((n,)),
        ],
        compiler_params=pltpu.CompilerParams(
            collective_id=0, has_side_effects=True, vmem_limit_bytes=48 * 2**20
        ),
    )(
        queries, keys_new, values_new, keys_cache, values_cache,
        query_frame.reshape(8, 128), context_frame.reshape(56, 128),
    )


def solution(mesh):
    return jax.shard_map(
        shards,
        mesh=mesh,
        in_specs=(
            P(("rep", "blk", "uly"), None),
            P(("rep", "blk", "uly"), None),
            P(("rep", "blk", "uly"), None),
            P(("rep", "blk"), "uly"),
            P(("rep", "blk"), "uly"),
            P("rep"),
            P("rep"),
        ),
        out_specs=P(("rep", "blk", "uly"), None),
        check_vma=False,
    )
```

```python
import functools
import math

import jax
import jax.numpy as jnp
from jax import lax
from jax.experimental import pallas as pl
from jax.experimental.pallas import tpu as pltpu
from jax.sharding import PartitionSpec as P

HD = 128
NX, NZ, NU = 4, 8, 4
TOK = 8
CTXB = 224
NEWB = NU * TOK
KB = CTXB + NEWB
HEADS = 6
SCALE = math.log2(math.e) / math.sqrt(HD)
LOW = -1e30
MESH = pl.DeviceIdType.MESH
F32, BF16 = jnp.float32, jnp.bfloat16


def pair_start(x):
    return 3 * (x // 2) + lax.rem(x, 2)


def kernel(
    q_ref, kn_ref, vn_ref, kc_ref, vc_ref, qf_hbm, cf_hbm, out_ref,
    qf_ref, cf_ref,    qland, nland, vland, npair, vpair, qall, kbuf, vbuf, vt, sbuf, kft, qfr, osend, orecv, fsend, frecv,
    fr_sem, qs, qr, ns, nr, vs, vr, zs, zr, ps, pr, ks, kr, os, orr, fs, fr,
):
    blk, u = lax.axis_index("blk"), lax.axis_index("uly")
    x, z = blk // NZ, lax.rem(blk, NZ)
    me = x * NU + u
    slot = lax.rem(z, 2)
    lane = pl.multiple_of(slot * HD, HD)
    other = z + 1 - 2 * slot
    base = z - slot
    even = lax.rem(x + z, 2) == 0
    role = lax.rem(x + z, 2)

    def at(x_, z_, u_):
        return {"blk": x_ * NZ + z_, "uly": u_}

    def plane(i):
        dx, du = i // NU, i % NU
        return lax.rem(x + dx, NX), lax.rem(u + du, NU)

    def along(k):
        return at(x, lax.rem(z + NZ - k, NZ), u)

    frame_copies = [
        pltpu.make_async_copy(qf_hbm, qf_ref, fr_sem.at[0]),
        pltpu.make_async_copy(cf_hbm, cf_ref, fr_sem.at[1]),
    ]
    for copy in frame_copies:
        copy.start()

    barrier = pltpu.get_barrier_semaphore()
    for i in range(1, NX * NU):
        px, pu = plane(i)
        pl.semaphore_signal(barrier, inc=1, device_id=at(px, z, pu), device_id_type=MESH)
    for k in range(1, NZ):
        pl.semaphore_signal(barrier, inc=1, device_id=along(k), device_id_type=MESH)
    for step in range(1, NX):
        pl.semaphore_signal(
            barrier, inc=1, device_id=at(lax.rem(x + step, NX), other, u), device_id_type=MESH
        )
    pl.semaphore_wait(barrier, NX * NU - 1 + NZ - 1 + NX - 1)

    def columns(px, pu):
        return pl.ds(pl.multiple_of((HEADS * pu + pair_start(px)) * HD, HD), 2 * HD)

    def small(src, dst, ssem, rsem):
        copies = []
        for i in range(1, NX * NU):
            px, pu = plane(i)
            copies.append(
                pltpu.make_async_remote_copy(
                    src_ref=src.at[:, columns(px, pu)],
                    dst_ref=dst.at[me],
                    send_sem=ssem.at[i],
                    recv_sem=rsem.at[me],
                    device_id=at(px, z, pu),
                    device_id_type=MESH,
                )
            )
            copies[-1].start()
        pltpu.make_async_copy(src.at[:, columns(x, u)], dst.at[me], rsem.at[me]).start()
        return copies

    def landed(dst, rsem):
        for i in range(NX * NU):
            pltpu.make_async_copy(dst.at[i], dst.at[i], rsem.at[i]).wait()

    sends = small(q_ref, qland, qs, qr)

    caches = ((0, kc_ref, kbuf), (1, vc_ref, vbuf))

    def cached(px, pz, ssem):
        mine = lax.rem(z, 2)
        whole = lax.rem(px + pz, 2) == 0
        far = (x != px).astype(jnp.int32)
        dst = jnp.where(whole, mine * NX + x, mine * 2 + far)
        copies = []
        for i, ref, buf in caches:
            src = ref.at[:, pl.ds(pl.multiple_of((pair_start(px) + lax.rem(pz, 2)) * HD, HD), HD)]
            copies.append(
                pltpu.make_async_remote_copy(
                    src_ref=src,
                    dst_ref=buf.at[dst, pl.ds(0, CTXB)],
                    send_sem=ks.at[i, ssem],
                    recv_sem=kr.at[i, dst],
                    device_id=at(px, pz, u),
                    device_id_type=MESH,
                )
            )
        return copies

    def takes(px, pz):
        return (lax.rem(px + pz, 2) == 0) | (px == x) | (px == NX - 1 - x)

    for step in (2, 1, 3, 0):
        px = lax.rem(x + step, NX)
        for n, pz in enumerate((other, z)):
            if step == 0 and n == 1:
                continue

            @pl.when(takes(px, pz))
            def _():
                for copy in cached(px, pz, 2 * step + n):
                    copy.start()

    own_slot = jnp.where(even, slot * NX + x, slot * 2)
    for i, ref, buf in caches:
        pltpu.make_async_copy(
            ref.at[:, pl.ds(pl.multiple_of((pair_start(x) + slot) * HD, HD), HD)],
            buf.at[own_slot, pl.ds(0, CTXB)],
            kr.at[i, own_slot],
        ).start()

    sends += small(kn_ref, nland, ns, nr)
    sends += small(vn_ref, vland, vs, vr)

    for copy in frame_copies:
        copy.wait()
    lanes = lax.broadcasted_iota(jnp.int32, (1, 128), 1)
    for zz in range(NZ):
        row = jnp.zeros((1, 128), jnp.int32)
        for xx in range(NX):
            part = qf_ref[pl.ds(2 * xx + zz // 4, 1), :]
            part = pltpu.roll(part, (xx * 32 - (zz % 4) * 32) % 128, 1)
            row = jnp.where(lanes // 32 == xx, part, row)
        qfr[zz] = jnp.broadcast_to(row, (8, 128))
    for block in range(2 * NX):
        xx, bz = block % NX, base + block // NX
        place = (xx * NZ + bz) * CTXB
        first, off = place // 128, lax.rem(place, 128)
        rows = [
            pltpu.roll(
                jnp.broadcast_to(cf_ref[pl.ds(jnp.minimum(first + j, 55), 1), :], (8, 128)),
                lax.rem(128 - off, 128),
                1,
            )
            for j in range(3)
        ]
        lanes8 = lax.broadcasted_iota(jnp.int32, (8, 128), 1)
        low = jnp.where(lanes8 < 128 - off, rows[0], rows[1])
        high = jnp.where(lanes8 < 128 - off, rows[1], rows[2])
        token = (xx * NZ + bz) * NEWB
        new = jnp.broadcast_to(qf_ref[pl.ds(token // 128, 1), :], (8, 128))
        new = pltpu.roll(new, lax.rem(96 + 128 - lax.rem(token, 128), 128), 1)
        high = jnp.where(lanes8 >= 96, new, high)
        for h, part in enumerate((low, high)):
            wide = jnp.broadcast_to(part[:1].astype(F32), (128, 128))
            kft[block, pl.ds(h * 128, 128), :] = wide.T.astype(jnp.int32)

    landed(qland, qr)
    for k in (1, 7, 2, 6, 3, 5, 4):
        pz = lax.rem(z + k, NZ)
        copy = pltpu.make_async_remote_copy(
            src_ref=qland.at[:, :, pl.ds(pl.multiple_of(lax.rem(pz, 2) * HD, HD), HD)],
            dst_ref=qall.at[k],
            send_sem=zs.at[k],
            recv_sem=zr.at[k],
            device_id=at(x, pz, u),
            device_id_type=MESH,
        )
        copy.start()
        sends.append(copy)
    qall[0] = qland[:, :, pl.ds(lane, HD)]

    landed(nland, nr)
    landed(vland, vr)
    lands = ((0, nland, npair, kbuf), (1, vland, vpair, vbuf))
    for i, land, pair, _ in lands:
        copy = pltpu.make_async_remote_copy(
            src_ref=land.at[:, :, pl.ds(pl.multiple_of((1 - slot) * HD, HD), HD)],
            dst_ref=pair,
            send_sem=ps.at[i],
            recv_sem=pr.at[i],
            device_id=at(x, other, u),
            device_id_type=MESH,
        )
        copy.start()
        sends.append(copy)
    for i, _, pair, _ in lands:
        pltpu.make_async_copy(pair, pair, pr.at[i]).wait()

    def join(dst, xx, mine):
        for i, land, pair, buf in lands:
            rows = buf.at[dst, pl.ds(0, CTXB)]
            pltpu.make_async_copy(rows, rows, kr.at[i, dst]).wait()
            here = land[pl.ds(xx * NU, NU), :, pl.ds(lane, HD)]
            there = pair[pl.ds(xx * NU, NU)]
            new = jnp.where(mine, here.astype(F32), there.astype(F32))
            buf[dst, pl.ds(CTXB, NEWB), :] = new.reshape(NEWB, HD).astype(BF16)
        vt[dst] = vbuf[dst].T

    def order(i):
        odd = lax.rem(i, 2)
        return odd * ((i + 1) // 2) + (1 - odd) * lax.rem(NZ - i // 2, NZ)

    def attend(blocks, i):
        k = order(i)

        @pl.when(k > 0)
        def _():
            pltpu.make_async_copy(qall.at[k], qall.at[k], zr.at[k]).wait()

        zz = lax.rem(z + NZ - k, NZ)
        query = qall[k].astype(F32).reshape(NX * NU * TOK, HD).astype(BF16)
        frames = qfr[zz][:1]
        top = jnp.full((8, 128), LOW, F32)
        for dst, block in blocks:
            s = lax.dot_general(
                kbuf[dst], query, (((1,), (1,)), ((), ())), preferred_element_type=F32
            )
            s = jnp.where(kft[block] <= frames, s * SCALE, LOW)
            sbuf[dst] = s
            top = jnp.maximum(top, jnp.max(s.reshape(KB // 8, 8, 128), axis=0))
        top = jnp.max(top, axis=0, keepdims=True)
        total = jnp.zeros((8, 128), F32)
        summed = jnp.zeros((HD, 128), F32)
        for dst, _ in blocks:
            w = jnp.exp2(sbuf[dst] - top)
            total += jnp.sum(w.reshape(KB // 8, 8, 128), axis=0)
            summed += jnp.dot(vt[dst], w.astype(BF16), preferred_element_type=F32)
        total = jnp.sum(total, axis=0, keepdims=True)
        osend[k, pl.ds(0, HD), :] = (summed / total).astype(BF16)
        level = top + jnp.log2(total)
        one = level.astype(BF16).astype(F32)
        two = (level - one).astype(BF16).astype(F32)
        three = level - one - two
        row = lax.broadcasted_iota(jnp.int32, (16, 128), 0)
        rows = jnp.where(row == 0, one, jnp.where(row == 1, two, jnp.where(row == 2, three, 0.0)))
        osend[k, pl.ds(HD, 16), :] = rows.astype(BF16)

        @pl.when(k > 0)
        def _():
            pltpu.make_async_remote_copy(
                src_ref=osend.at[k],
                dst_ref=orecv.at[k],
                send_sem=os.at[k],
                recv_sem=orr.at[k],
                device_id=along(k),
                device_id_type=MESH,
            ).start()

    def work(blocks):
        for dst, block in blocks:
            xx = lax.rem(block, NX)
            join(dst, xx, block // NX == slot)

        def chunk(i, carry):
            attend(blocks, i)
            return carry

        lax.fori_loop(0, NZ, chunk, 0)

    @pl.when(even)
    def _():
        work([(b, b) for b in range(2 * NX)])

    @pl.when(jnp.logical_not(even))
    def _():
        work([(2 * b + f, b * NX + (x if f == 0 else NX - 1 - x)) for b in range(2) for f in range(2)])

    orecv[0] = osend[0]

    for k in range(1, NZ):
        pltpu.make_async_copy(orecv.at[k], orecv.at[k], orr.at[k]).wait()

    def merge(kind):
        parity = lax.rem(role + kind, 2)
        parts = [orecv.at[2 * j + parity] for j in range(NZ // 2)]
        levels = []
        for part in parts:
            tail = part[pl.ds(HD, 16), :].astype(F32)
            levels.append(tail[0:1] + tail[1:2] + tail[2:3])
        top = functools.reduce(jnp.maximum, levels)
        weights = [jnp.exp2(level - top) for level in levels]
        total = functools.reduce(jnp.add, weights)
        merged = jnp.zeros((HD, 128), F32)
        for part, w in zip(parts, weights):
            merged += part[pl.ds(0, HD), :].astype(F32) * w
        return merged / total, top + jnp.log2(total)

    merged, level = merge(1)
    fsend[:, pl.ds(TOK, TOK), :] = merged.T.reshape(NX * NU, TOK, HD)
    fsend[:, pl.ds(2 * TOK, TOK), :] = jnp.broadcast_to(level, (128, 128)).T.reshape(
        NX * NU, TOK, HD
    )
    merged, _ = merge(0)
    fsend[:, pl.ds(0, TOK), :] = merged.T.reshape(NX * NU, TOK, HD)

    for i in range(1, NX * NU):
        px, pu = plane(i)
        copy = pltpu.make_async_remote_copy(
            src_ref=fsend.at[px * NU + pu],
            dst_ref=frecv.at[me],
            send_sem=fs.at[i],
            recv_sem=fr.at[me],
            device_id=at(px, z, pu),
            device_id_type=MESH,
        )
        copy.start()
        sends.append(copy)
    pltpu.make_async_copy(fsend.at[me], frecv.at[me], fr.at[me]).start()
    landed(frecv, fr)
    for uu in range(NU):
        for half in range(2):
            ends = (frecv.at[2 * half * NU + uu], frecv.at[(2 * half + 1) * NU + uu])
            base = (HEADS * uu + 3 * half) * HD
            for e, end in enumerate(ends):
                out_ref[:, pl.ds(base + 2 * e * HD, HD)] = end[pl.ds(0, TOK), :].astype(BF16)
            levels = [end[pl.ds(2 * TOK, TOK), :] for end in ends]
            top = jnp.maximum(levels[0], levels[1])
            w = [jnp.exp2(level - top) for level in levels]
            both = [end[pl.ds(TOK, TOK), :] for end in ends]
            mixed = (both[0] * w[0] + both[1] * w[1]) / (w[0] + w[1])
            out_ref[:, pl.ds(base + HD, HD)] = mixed.astype(BF16)

    for copy in sends:
        copy.wait_send()
    for step in range(NX):
        px = lax.rem(x + step, NX)
        for n, pz in enumerate((other, z)):
            if step == 0 and n == 1:
                continue

            @pl.when(takes(px, pz))
            def _():
                for copy in cached(px, pz, 2 * step + n):
                    copy.wait_send()

    for k in range(1, NZ):
        pltpu.make_async_copy(osend.at[k], osend.at[k], os.at[k]).wait()


def shards(queries, keys_new, values_new, keys_cache, values_cache, query_frame, context_frame):
    hbm = pl.BlockSpec(memory_space=pltpu.HBM)
    vmem = pl.BlockSpec(memory_space=pltpu.VMEM)
    dma = pltpu.SemaphoreType.DMA
    n = NX * NU
    return pl.pallas_call(
        kernel,
        out_shape=jax.ShapeDtypeStruct((TOK, queries.shape[1]), BF16),
        in_specs=[hbm] * 7,
        out_specs=vmem,
        scratch_shapes=[
            pltpu.VMEM((8, 128), jnp.int32),
            pltpu.VMEM((56, 128), jnp.int32),
            pltpu.VMEM((n, TOK, 2 * HD), BF16),
            pltpu.VMEM((n, TOK, 2 * HD), BF16),
            pltpu.VMEM((n, TOK, 2 * HD), BF16),
            pltpu.VMEM((n, TOK, HD), BF16),
            pltpu.VMEM((n, TOK, HD), BF16),
            pltpu.VMEM((NZ, n, TOK, HD), BF16),
            pltpu.VMEM((2 * NX, KB, HD), BF16),
            pltpu.VMEM((2 * NX, KB, HD), BF16),
            pltpu.VMEM((2 * NX, HD, KB), BF16),
            pltpu.VMEM((2 * NX, KB, 128), F32),
            pltpu.VMEM((2 * NX, KB, 128), jnp.int32),
            pltpu.VMEM((NZ, 8, 128), jnp.int32),
            pltpu.VMEM((NZ, HD + 16, 128), BF16),
            pltpu.VMEM((NZ, HD + 16, 128), BF16),
            pltpu.VMEM((n, 3 * TOK, HD), F32),
            pltpu.VMEM((n, 3 * TOK, HD), F32),
            dma((2,)),
            dma((n,)), dma((n,)), dma((n,)), dma((n,)), dma((n,)), dma((n,)),
            dma((NZ,)), dma((NZ,)),
            dma((2,)), dma((2,)),
            dma((2, 2 * NX)), dma((2, 2 * NX)),
            dma((NZ,)), dma((NZ,)),
            dma((n,)), dma((n,)),
        ],
        compiler_params=pltpu.CompilerParams(
            collective_id=0, has_side_effects=True, vmem_limit_bytes=64 * 2**20
        ),
    )(
        queries, keys_new, values_new, keys_cache, values_cache,
        query_frame.reshape(8, 128), context_frame.reshape(56, 128),
    )


def solution(mesh):
    return jax.shard_map(
        shards,
        mesh=mesh,
        in_specs=(
            P(("rep", "blk", "uly"), None),
            P(("rep", "blk", "uly"), None),
            P(("rep", "blk", "uly"), None),
            P(("rep", "blk"), "uly"),
            P(("rep", "blk"), "uly"),
            P("rep"),
            P("rep"),
        ),
        out_specs=P(("rep", "blk", "uly"), None),
        check_vma=False,
    )
```

```python
import functools
import math

import jax
import jax.numpy as jnp
from jax import lax
from jax.experimental import pallas as pl
from jax.experimental.pallas import tpu as pltpu
from jax.sharding import PartitionSpec as P

HD = 128
NX, NZ, NU = 4, 8, 4
TOK = 8
CTXB = 224
NEWB = NU * TOK
KB = CTXB + NEWB
HEADS = 6
SCALE = math.log2(math.e) / math.sqrt(HD)
LOW = -1e30
MESH = pl.DeviceIdType.MESH
F32, BF16 = jnp.float32, jnp.bfloat16


def pair_start(x):
    return 3 * (x // 2) + lax.rem(x, 2)


def kernel(
    q_ref, kn_ref, vn_ref, kc_ref, vc_ref, qf_hbm, cf_hbm, out_ref,
    qf_ref, cf_ref,    stage, qland, nland, qall, kbuf, vbuf, vt, sbuf, kft, qfr, osend, orecv, fsend, frecv,
    st, fr_sem, qs, qr, ns, nr, zs, zr, ks, kr, os, orr, fs, fr,
):
    blk, u = lax.axis_index("blk"), lax.axis_index("uly")
    x, z = blk // NZ, lax.rem(blk, NZ)
    me = x * NU + u
    slot = lax.rem(z, 2)
    other = z + 1 - 2 * slot
    base = z - slot
    even = lax.rem(x + z, 2) == 0
    role = lax.rem(x + z, 2)

    def at(x_, z_, u_):
        return {"blk": x_ * NZ + z_, "uly": u_}

    def plane(i):
        dx, du = i // NU, i % NU
        return lax.rem(x + dx, NX), lax.rem(u + du, NU)

    def along(k):
        return at(x, lax.rem(z + NZ - k, NZ), u)

    staged = [
        pltpu.make_async_copy(ref, stage.at[i], st.at[i])
        for i, ref in enumerate((q_ref, kn_ref, vn_ref))
    ]
    frame_copies = [
        pltpu.make_async_copy(qf_hbm, qf_ref, fr_sem.at[0]),
        pltpu.make_async_copy(cf_hbm, cf_ref, fr_sem.at[1]),
    ]
    for copy in staged + frame_copies:
        copy.start()

    barrier = pltpu.get_barrier_semaphore()
    for i in range(1, NX * NU):
        px, pu = plane(i)
        pl.semaphore_signal(barrier, inc=1, device_id=at(px, z, pu), device_id_type=MESH)
    for k in range(1, NZ):
        pl.semaphore_signal(barrier, inc=1, device_id=along(k), device_id_type=MESH)
    for i in range(1, NX * NU):
        px, pu = plane(i)
        pl.semaphore_signal(barrier, inc=1, device_id=at(px, other, pu), device_id_type=MESH)
    pl.semaphore_wait(barrier, 2 * (NX * NU - 1) + NZ - 1)
    for copy in staged:
        copy.wait()

    def remote(src, dst, ssem, rsem, px, pz, pu):
        return pltpu.make_async_remote_copy(
            src_ref=src,
            dst_ref=dst,
            send_sem=ssem,
            recv_sem=rsem,
            device_id=at(px, pz, pu),
            device_id_type=MESH,
        )

    def heads(px, pu):
        return HEADS * pu + pair_start(px)

    sends = []
    for i in range(1, NX * NU):
        px, pu = plane(i)
        src = stage.at[0, pl.ds(heads(px, pu), 2)]
        sends.append(remote(src, qland.at[:, me], qs.at[i], qr.at[me], px, z, pu))
    for n, pz in enumerate((z, other)):
        for i in range(1 - n, NX * NU):
            px, pu = plane(i)
            src = stage.at[pl.ds(1, 2), heads(px, pu) + lax.rem(pz, 2)]
            dst = nland.at[slot, :, me]
            sends.append(remote(src, dst, ns.at[n, i], nr.at[slot, me], px, pz, pu))
    for copy in sends:
        copy.start()
    pltpu.make_async_copy(stage.at[0, pl.ds(heads(x, u), 2)], qland.at[:, me], qr.at[me]).start()
    pltpu.make_async_copy(
        stage.at[pl.ds(1, 2), heads(x, u) + slot], nland.at[slot, :, me], nr.at[slot, me]
    ).start()

    def landed(dst, rsem, count=NX * NU):
        for i in range(count):
            pltpu.make_async_copy(dst(i), dst(i), rsem.at[i]).wait()

    caches = ((0, kc_ref, kbuf), (1, vc_ref, vbuf))

    def cached(px, pz, ssem):
        mine = lax.rem(z, 2)
        whole = lax.rem(px + pz, 2) == 0
        far = (x != px).astype(jnp.int32)
        dst = jnp.where(whole, mine * NX + x, mine * 2 + far)
        copies = []
        for i, ref, buf in caches:
            src = ref.at[:, pl.ds(pl.multiple_of((pair_start(px) + lax.rem(pz, 2)) * HD, HD), HD)]
            copies.append(
                pltpu.make_async_remote_copy(
                    src_ref=src,
                    dst_ref=buf.at[dst, pl.ds(0, CTXB)],
                    send_sem=ks.at[i, ssem],
                    recv_sem=kr.at[i, dst],
                    device_id=at(px, pz, u),
                    device_id_type=MESH,
                )
            )
        return copies

    def takes(px, pz):
        return (lax.rem(px + pz, 2) == 0) | (px == x) | (px == NX - 1 - x)

    for step in (2, 1, 3, 0):
        px = lax.rem(x + step, NX)
        for n, pz in enumerate((other, z)):
            if step == 0 and n == 1:
                continue

            @pl.when(takes(px, pz))
            def _():
                for copy in cached(px, pz, 2 * step + n):
                    copy.start()

    own_slot = jnp.where(even, slot * NX + x, slot * 2)
    for i, ref, buf in caches:
        pltpu.make_async_copy(
            ref.at[:, pl.ds(pl.multiple_of((pair_start(x) + slot) * HD, HD), HD)],
            buf.at[own_slot, pl.ds(0, CTXB)],
            kr.at[i, own_slot],
        ).start()

    for copy in frame_copies:
        copy.wait()
    lanes = lax.broadcasted_iota(jnp.int32, (1, 128), 1)
    for zz in range(NZ):
        row = jnp.zeros((1, 128), jnp.int32)
        for xx in range(NX):
            part = qf_ref[pl.ds(2 * xx + zz // 4, 1), :]
            part = pltpu.roll(part, (xx * 32 - (zz % 4) * 32) % 128, 1)
            row = jnp.where(lanes // 32 == xx, part, row)
        qfr[zz] = jnp.broadcast_to(row, (8, 128))
    for block in range(2 * NX):
        xx, bz = block % NX, base + block // NX
        place = (xx * NZ + bz) * CTXB
        first, off = place // 128, lax.rem(place, 128)
        rows = [
            pltpu.roll(
                jnp.broadcast_to(cf_ref[pl.ds(jnp.minimum(first + j, 55), 1), :], (8, 128)),
                lax.rem(128 - off, 128),
                1,
            )
            for j in range(3)
        ]
        lanes8 = lax.broadcasted_iota(jnp.int32, (8, 128), 1)
        low = jnp.where(lanes8 < 128 - off, rows[0], rows[1])
        high = jnp.where(lanes8 < 128 - off, rows[1], rows[2])
        token = (xx * NZ + bz) * NEWB
        new = jnp.broadcast_to(qf_ref[pl.ds(token // 128, 1), :], (8, 128))
        new = pltpu.roll(new, lax.rem(96 + 128 - lax.rem(token, 128), 128), 1)
        high = jnp.where(lanes8 >= 96, new, high)
        for h, part in enumerate((low, high)):
            wide = jnp.broadcast_to(part[:1].astype(F32), (128, 128))
            kft[block, pl.ds(h * 128, 128), :] = wide.T.astype(jnp.int32)

    landed(lambda i: qland.at[:, i], qr)
    for k in (1, 7, 2, 6, 3, 5, 4):
        pz = lax.rem(z + k, NZ)
        copy = remote(qland.at[lax.rem(pz, 2)], qall.at[k], zs.at[k], zr.at[k], x, pz, u)
        copy.start()
        sends.append(copy)
    qall[0] = qland[slot]

    for p in range(2):
        landed(lambda i: nland.at[p, :, i], nr.at[p])

    def join(dst, xx, p):
        for i, buf in enumerate((kbuf, vbuf)):
            rows = buf.at[dst, pl.ds(0, CTXB)]
            pltpu.make_async_copy(rows, rows, kr.at[i, dst]).wait()
            new = nland[p, i, pl.ds(xx * NU, NU)].astype(F32).reshape(NEWB, HD)
            buf[dst, pl.ds(CTXB, NEWB), :] = new.astype(BF16)
        vt[dst] = vbuf[dst].T

    def order(i):
        odd = lax.rem(i, 2)
        return odd * ((i + 1) // 2) + (1 - odd) * lax.rem(NZ - i // 2, NZ)

    def attend(blocks, i):
        k = order(i)

        @pl.when(k > 0)
        def _():
            pltpu.make_async_copy(qall.at[k], qall.at[k], zr.at[k]).wait()

        zz = lax.rem(z + NZ - k, NZ)
        query = qall[k].astype(F32).reshape(NX * NU * TOK, HD).astype(BF16)
        frames = qfr[zz][:1]
        top = jnp.full((8, 128), LOW, F32)
        for dst, block in blocks:
            s = lax.dot_general(
                kbuf[dst], query, (((1,), (1,)), ((), ())), preferred_element_type=F32
            )
            s = jnp.where(kft[block] <= frames, s * SCALE, LOW)
            sbuf[dst] = s
            top = jnp.maximum(top, jnp.max(s.reshape(KB // 8, 8, 128), axis=0))
        top = jnp.max(top, axis=0, keepdims=True)
        total = jnp.zeros((8, 128), F32)
        summed = jnp.zeros((HD, 128), F32)
        for dst, _ in blocks:
            w = jnp.exp2(sbuf[dst] - top)
            total += jnp.sum(w.reshape(KB // 8, 8, 128), axis=0)
            summed += jnp.dot(vt[dst], w.astype(BF16), preferred_element_type=F32)
        total = jnp.sum(total, axis=0, keepdims=True)
        osend[k, pl.ds(0, HD), :] = (summed / total).astype(BF16)
        level = top + jnp.log2(total)
        one = level.astype(BF16).astype(F32)
        two = (level - one).astype(BF16).astype(F32)
        three = level - one - two
        row = lax.broadcasted_iota(jnp.int32, (16, 128), 0)
        rows = jnp.where(row == 0, one, jnp.where(row == 1, two, jnp.where(row == 2, three, 0.0)))
        osend[k, pl.ds(HD, 16), :] = rows.astype(BF16)

        @pl.when(k > 0)
        def _():
            pltpu.make_async_remote_copy(
                src_ref=osend.at[k],
                dst_ref=orecv.at[k],
                send_sem=os.at[k],
                recv_sem=orr.at[k],
                device_id=along(k),
                device_id_type=MESH,
            ).start()

    def work(blocks):
        for dst, block in blocks:
            xx = lax.rem(block, NX)
            join(dst, xx, block // NX)

        def chunk(i, carry):
            attend(blocks, i)
            return carry

        lax.fori_loop(0, NZ, chunk, 0)

    @pl.when(even)
    def _():
        work([(b, b) for b in range(2 * NX)])

    @pl.when(jnp.logical_not(even))
    def _():
        work([(2 * b + f, b * NX + (x if f == 0 else NX - 1 - x)) for b in range(2) for f in range(2)])

    orecv[0] = osend[0]

    for k in range(1, NZ):
        pltpu.make_async_copy(orecv.at[k], orecv.at[k], orr.at[k]).wait()

    def merge(kind):
        parity = lax.rem(role + kind, 2)
        parts = [orecv.at[2 * j + parity] for j in range(NZ // 2)]
        levels = []
        for part in parts:
            tail = part[pl.ds(HD, 16), :].astype(F32)
            levels.append(tail[0:1] + tail[1:2] + tail[2:3])
        top = functools.reduce(jnp.maximum, levels)
        weights = [jnp.exp2(level - top) for level in levels]
        total = functools.reduce(jnp.add, weights)
        merged = jnp.zeros((HD, 128), F32)
        for part, w in zip(parts, weights):
            merged += part[pl.ds(0, HD), :].astype(F32) * w
        return merged / total, top + jnp.log2(total)

    merged, level = merge(1)
    fsend[:, 1] = merged.T.reshape(NX * NU, TOK, HD).astype(BF16)
    one = level.astype(BF16).astype(F32)
    two = (level - one).astype(BF16).astype(F32)
    three = level - one - two
    row = lax.broadcasted_iota(jnp.int32, (128, 128), 0)
    level = jnp.where(row == 0, one, jnp.where(row == 1, two, jnp.where(row == 2, three, 0.0)))
    fsend[:, 2] = level.T.reshape(NX * NU, TOK, HD).astype(BF16)
    merged, _ = merge(0)
    fsend[:, 0] = merged.T.reshape(NX * NU, TOK, HD).astype(BF16)

    for i in range(1, NX * NU):
        px, pu = plane(i)
        copy = remote(fsend.at[px * NU + pu], frecv.at[me], fs.at[i], fr.at[me], px, z, pu)
        copy.start()
        sends.append(copy)
    pltpu.make_async_copy(fsend.at[me], frecv.at[me], fr.at[me]).start()
    landed(lambda i: frecv.at[i], fr)
    for uu in range(NU):
        for half in range(2):
            ends = (frecv.at[2 * half * NU + uu], frecv.at[(2 * half + 1) * NU + uu])
            head = HEADS * uu + 3 * half
            out_ref[head] = ends[0][0]
            out_ref[head + 2] = ends[1][0]
            levels = []
            for end in ends:
                tail = end[2].astype(F32)
                levels.append(tail[:, 0:1] + tail[:, 1:2] + tail[:, 2:3])
            top = jnp.maximum(levels[0], levels[1])
            w = [jnp.exp2(level - top) for level in levels]
            both = [end[1].astype(F32) for end in ends]
            mixed = (both[0] * w[0] + both[1] * w[1]) / (w[0] + w[1])
            out_ref[head + 1] = mixed.astype(BF16)

    for copy in sends:
        copy.wait_send()
    for step in range(NX):
        px = lax.rem(x + step, NX)
        for n, pz in enumerate((other, z)):
            if step == 0 and n == 1:
                continue

            @pl.when(takes(px, pz))
            def _():
                for copy in cached(px, pz, 2 * step + n):
                    copy.wait_send()

    for k in range(1, NZ):
        pltpu.make_async_copy(osend.at[k], osend.at[k], os.at[k]).wait()


def shards(queries, keys_new, values_new, keys_cache, values_cache, query_frame, context_frame):
    hbm = pl.BlockSpec(memory_space=pltpu.HBM)
    vmem = pl.BlockSpec(memory_space=pltpu.VMEM)
    dma = pltpu.SemaphoreType.DMA
    n = NX * NU

    def by_head(rows):
        return rows.reshape(TOK, NU * HEADS, HD).transpose(1, 0, 2)

    out = pl.pallas_call(
        kernel,
        out_shape=jax.ShapeDtypeStruct((NU * HEADS, TOK, HD), BF16),
        in_specs=[hbm] * 7,
        out_specs=vmem,
        scratch_shapes=[
            pltpu.VMEM((8, 128), jnp.int32),
            pltpu.VMEM((56, 128), jnp.int32),
            pltpu.VMEM((3, NU * HEADS, TOK, HD), BF16),
            pltpu.VMEM((2, n, TOK, HD), BF16),
            pltpu.VMEM((2, 2, n, TOK, HD), BF16),
            pltpu.VMEM((NZ, n, TOK, HD), BF16),
            pltpu.VMEM((2 * NX, KB, HD), BF16),
            pltpu.VMEM((2 * NX, KB, HD), BF16),
            pltpu.VMEM((2 * NX, HD, KB), BF16),
            pltpu.VMEM((2 * NX, KB, 128), F32),
            pltpu.VMEM((2 * NX, KB, 128), jnp.int32),
            pltpu.VMEM((NZ, 8, 128), jnp.int32),
            pltpu.VMEM((NZ, HD + 16, 128), BF16),
            pltpu.VMEM((NZ, HD + 16, 128), BF16),
            pltpu.VMEM((n, 3, TOK, HD), BF16),
            pltpu.VMEM((n, 3, TOK, HD), BF16),
            dma((3,)), dma((2,)),
            dma((n,)), dma((n,)),
            dma((2, n)), dma((2, n)),
            dma((NZ,)), dma((NZ,)),
            dma((2, 2 * NX)), dma((2, 2 * NX)),
            dma((NZ,)), dma((NZ,)),
            dma((n,)), dma((n,)),
        ],
        compiler_params=pltpu.CompilerParams(
            collective_id=0, has_side_effects=True, vmem_limit_bytes=64 * 2**20
        ),
    )(
        by_head(queries), by_head(keys_new), by_head(values_new), keys_cache, values_cache,
        query_frame.reshape(8, 128), context_frame.reshape(56, 128),
    )
    return out.transpose(1, 0, 2).reshape(queries.shape)


def solution(mesh):
    return jax.shard_map(
        shards,
        mesh=mesh,
        in_specs=(
            P(("rep", "blk", "uly"), None),
            P(("rep", "blk", "uly"), None),
            P(("rep", "blk", "uly"), None),
            P(("rep", "blk"), "uly"),
            P(("rep", "blk"), "uly"),
            P("rep"),
            P("rep"),
        ),
        out_specs=P(("rep", "blk", "uly"), None),
        check_vma=False,
    )
```

```python
import functools
import math

import jax
import jax.numpy as jnp
from jax import lax
from jax.experimental import pallas as pl
from jax.experimental.pallas import tpu as pltpu
from jax.sharding import PartitionSpec as P

HD = 128
NX, NZ, NU = 4, 8, 4
TOK = 8
CTXB = 224
NEWB = NU * TOK
KB = CTXB + NEWB
HEADS = 6
SCALE = math.log2(math.e) / math.sqrt(HD)
LOW = -1e30
MESH = pl.DeviceIdType.MESH
F32, BF16 = jnp.float32, jnp.bfloat16


def pair_start(x):
    return 3 * (x // 2) + lax.rem(x, 2)


def kernel(
    q_ref, kn_ref, vn_ref, kc_ref, vc_ref, qf_hbm, cf_hbm, out_ref,
    qf_ref, cf_ref,    stage, cache, qland, nland, qall, kvbuf, vt, sbuf, kft, qfr, osend, orecv, fsend, frecv,
    st, ct, fr_sem, qs, qr, ns, nr, zs, zr, ks, kr, os, orr, fs, fr,
):
    blk, u = lax.axis_index("blk"), lax.axis_index("uly")
    x, z = blk // NZ, lax.rem(blk, NZ)
    me = x * NU + u
    slot = lax.rem(z, 2)
    other = z + 1 - 2 * slot
    base = z - slot
    even = lax.rem(x + z, 2) == 0
    role = lax.rem(x + z, 2)

    def at(x_, z_, u_):
        return {"blk": x_ * NZ + z_, "uly": u_}

    def plane(i):
        dx, du = i // NU, i % NU
        return lax.rem(x + dx, NX), lax.rem(u + du, NU)

    def along(k):
        return at(x, lax.rem(z + NZ - k, NZ), u)

    staged = [
        pltpu.make_async_copy(ref, stage.at[i], st.at[i])
        for i, ref in enumerate((q_ref, kn_ref, vn_ref))
    ]
    frame_copies = [
        pltpu.make_async_copy(qf_hbm, qf_ref, fr_sem.at[0]),
        pltpu.make_async_copy(cf_hbm, cf_ref, fr_sem.at[1]),
    ]
    cache_copies = [
        pltpu.make_async_copy(ref.at[:, pl.ds(h * HD, HD)], cache.at[h, i], ct.at[h, i])
        for h in range(HEADS)
        for i, ref in enumerate((kc_ref, vc_ref))
    ]
    for copy in staged + cache_copies + frame_copies:
        copy.start()

    barrier = pltpu.get_barrier_semaphore()
    for i in range(1, NX * NU):
        px, pu = plane(i)
        pl.semaphore_signal(barrier, inc=1, device_id=at(px, z, pu), device_id_type=MESH)
    for k in range(1, NZ):
        pl.semaphore_signal(barrier, inc=1, device_id=along(k), device_id_type=MESH)
    for i in range(1, NX * NU):
        px, pu = plane(i)
        pl.semaphore_signal(barrier, inc=1, device_id=at(px, other, pu), device_id_type=MESH)
    pl.semaphore_wait(barrier, 2 * (NX * NU - 1) + NZ - 1)
    for copy in staged:
        copy.wait()

    def remote(src, dst, ssem, rsem, px, pz, pu):
        return pltpu.make_async_remote_copy(
            src_ref=src,
            dst_ref=dst,
            send_sem=ssem,
            recv_sem=rsem,
            device_id=at(px, pz, pu),
            device_id_type=MESH,
        )

    def heads(px, pu):
        return HEADS * pu + pair_start(px)

    sends = []
    for i in range(1, NX * NU):
        px, pu = plane(i)
        src = stage.at[0, pl.ds(heads(px, pu), 2)]
        sends.append(remote(src, qland.at[:, me], qs.at[i], qr.at[me], px, z, pu))
    for n, pz in enumerate((z, other)):
        for i in range(1 - n, NX * NU):
            px, pu = plane(i)
            src = stage.at[pl.ds(1, 2), heads(px, pu) + lax.rem(pz, 2)]
            dst = nland.at[slot, :, me]
            sends.append(remote(src, dst, ns.at[n, i], nr.at[slot, me], px, pz, pu))
    for copy in sends:
        copy.start()
    pltpu.make_async_copy(stage.at[0, pl.ds(heads(x, u), 2)], qland.at[:, me], qr.at[me]).start()
    pltpu.make_async_copy(
        stage.at[pl.ds(1, 2), heads(x, u) + slot], nland.at[slot, :, me], nr.at[slot, me]
    ).start()

    def landed(dst, rsem, count=NX * NU):
        for i in range(count):
            pltpu.make_async_copy(dst(i), dst(i), rsem.at[i]).wait()

    def cached(px, pz, ssem):
        whole = lax.rem(px + pz, 2) == 0
        dst = jnp.where(whole, slot * NX + x, x)
        return remote(
            cache.at[pair_start(px) + lax.rem(pz, 2)],
            kvbuf.at[dst, :, pl.ds(0, CTXB)],
            ks.at[ssem],
            kr.at[dst],
            px,
            pz,
            u,
        )

    def takes(px, pz):
        return (lax.rem(px + pz, 2) == 0) | (pz == z)

    def to_plane(act, steps, n):
        for step in steps:
            px, pz = lax.rem(x + step, NX), (other, z)[n]

            @pl.when(takes(px, pz))
            def _():
                act(cached(px, pz, 2 * step + n))

    for copy in cache_copies:
        copy.wait()
    to_plane(lambda copy: copy.start(), (2, 1, 3, 0), 0)
    own_slot = jnp.where(even, slot * NX + x, x)
    pltpu.make_async_copy(
        cache.at[pair_start(x) + slot], kvbuf.at[own_slot, :, pl.ds(0, CTXB)], kr.at[own_slot]
    ).start()

    for copy in frame_copies:
        copy.wait()
    lanes = lax.broadcasted_iota(jnp.int32, (1, 128), 1)
    for zz in range(NZ):
        row = jnp.zeros((1, 128), jnp.int32)
        for xx in range(NX):
            part = qf_ref[pl.ds(2 * xx + zz // 4, 1), :]
            part = pltpu.roll(part, (xx * 32 - (zz % 4) * 32) % 128, 1)
            row = jnp.where(lanes // 32 == xx, part, row)
        qfr[zz] = jnp.broadcast_to(row, (8, 128))
    for block in range(2 * NX):
        xx, bz = block % NX, base + block // NX
        place = (xx * NZ + bz) * CTXB
        first, off = place // 128, lax.rem(place, 128)
        rows = [
            pltpu.roll(
                jnp.broadcast_to(cf_ref[pl.ds(jnp.minimum(first + j, 55), 1), :], (8, 128)),
                lax.rem(128 - off, 128),
                1,
            )
            for j in range(3)
        ]
        lanes8 = lax.broadcasted_iota(jnp.int32, (8, 128), 1)
        low = jnp.where(lanes8 < 128 - off, rows[0], rows[1])
        high = jnp.where(lanes8 < 128 - off, rows[1], rows[2])
        token = (xx * NZ + bz) * NEWB
        new = jnp.broadcast_to(qf_ref[pl.ds(token // 128, 1), :], (8, 128))
        new = pltpu.roll(new, lax.rem(96 + 128 - lax.rem(token, 128), 128), 1)
        high = jnp.where(lanes8 >= 96, new, high)
        for h, part in enumerate((low, high)):
            wide = jnp.broadcast_to(part[:1].astype(F32), (128, 128))
            kft[block, pl.ds(h * 128, 128), :] = wide.T.astype(jnp.int32)

    landed(lambda i: qland.at[:, i], qr)
    for k in (1, 7, 2, 6, 3, 5, 4):
        pz = lax.rem(z + k, NZ)
        copy = remote(qland.at[lax.rem(pz, 2)], qall.at[k], zs.at[k], zr.at[k], x, pz, u)
        copy.start()
        sends.append(copy)
    to_plane(lambda copy: copy.start(), (2, 1, 3), 1)
    qall[0] = qland[slot]

    for p in range(2):
        landed(lambda i: nland.at[p, :, i], nr.at[p])

    def join(dst, xx, p):
        rows = kvbuf.at[dst, :, pl.ds(0, CTXB)]
        pltpu.make_async_copy(rows, rows, kr.at[dst]).wait()
        for i in range(2):
            new = nland[p, i, pl.ds(xx * NU, NU)].astype(F32).reshape(NEWB, HD)
            kvbuf[dst, i, pl.ds(CTXB, NEWB), :] = new.astype(BF16)
        vt[dst] = kvbuf[dst, 1].T

    def order(i):
        odd = lax.rem(i, 2)
        return odd * lax.rem(4 + (i + 1) // 2, NZ) + (1 - odd) * (4 - i // 2)

    def attend(blocks, i):
        k = order(i)

        @pl.when(k > 0)
        def _():
            pltpu.make_async_copy(qall.at[k], qall.at[k], zr.at[k]).wait()

        zz = lax.rem(z + NZ - k, NZ)
        query = qall[k].astype(F32).reshape(NX * NU * TOK, HD).astype(BF16)
        frames = qfr[zz][:1]
        top = jnp.full((8, 128), LOW, F32)
        for dst, block in blocks:
            s = lax.dot_general(
                kvbuf[dst, 0], query, (((1,), (1,)), ((), ())), preferred_element_type=F32
            )
            s = jnp.where(kft[block] <= frames, s * SCALE, LOW)
            sbuf[dst] = s
            top = jnp.maximum(top, jnp.max(s.reshape(KB // 8, 8, 128), axis=0))
        top = jnp.max(top, axis=0, keepdims=True)
        total = jnp.zeros((8, 128), F32)
        summed = jnp.zeros((HD, 128), F32)
        for dst, _ in blocks:
            w = jnp.exp2(sbuf[dst] - top)
            total += jnp.sum(w.reshape(KB // 8, 8, 128), axis=0)
            summed += jnp.dot(vt[dst], w.astype(BF16), preferred_element_type=F32)
        total = jnp.sum(total, axis=0, keepdims=True)
        osend[k, pl.ds(0, HD), :] = (summed / total).astype(BF16)
        level = top + jnp.log2(total)
        one = level.astype(BF16).astype(F32)
        two = (level - one).astype(BF16).astype(F32)
        three = level - one - two
        row = lax.broadcasted_iota(jnp.int32, (16, 128), 0)
        rows = jnp.where(row == 0, one, jnp.where(row == 1, two, jnp.where(row == 2, three, 0.0)))
        osend[k, pl.ds(HD, 16), :] = rows.astype(BF16)

        @pl.when(k > 0)
        def _():
            pltpu.make_async_remote_copy(
                src_ref=osend.at[k],
                dst_ref=orecv.at[k],
                send_sem=os.at[k],
                recv_sem=orr.at[k],
                device_id=along(k),
                device_id_type=MESH,
            ).start()

    def work(blocks):
        for dst, block in blocks:
            xx = lax.rem(block, NX)
            join(dst, xx, block // NX)

        def chunk(i, carry):
            attend(blocks, i)
            return carry

        lax.fori_loop(0, NZ, chunk, 0)

    @pl.when(even)
    def _():
        work([(b, b) for b in range(2 * NX)])

    @pl.when(jnp.logical_not(even))
    def _():
        work([(b, slot * NX + b) for b in range(NX)])

    orecv[0] = osend[0]

    for k in range(1, NZ):
        pltpu.make_async_copy(orecv.at[k], orecv.at[k], orr.at[k]).wait()

    def merge(kind):
        parity = lax.rem(role + kind, 2)
        parts = [orecv.at[2 * j + parity] for j in range(NZ // 2)]
        levels = []
        for part in parts:
            tail = part[pl.ds(HD, 16), :].astype(F32)
            levels.append(tail[0:1] + tail[1:2] + tail[2:3])
        top = functools.reduce(jnp.maximum, levels)
        weights = [jnp.exp2(level - top) for level in levels]
        total = functools.reduce(jnp.add, weights)
        merged = jnp.zeros((HD, 128), F32)
        for part, w in zip(parts, weights):
            merged += part[pl.ds(0, HD), :].astype(F32) * w
        return merged / total, top + jnp.log2(total)

    merged, level = merge(1)
    fsend[:, 1] = merged.T.reshape(NX * NU, TOK, HD).astype(BF16)
    one = level.astype(BF16).astype(F32)
    two = (level - one).astype(BF16).astype(F32)
    three = level - one - two
    row = lax.broadcasted_iota(jnp.int32, (128, 128), 0)
    level = jnp.where(row == 0, one, jnp.where(row == 1, two, jnp.where(row == 2, three, 0.0)))
    fsend[:, 2] = level.T.reshape(NX * NU, TOK, HD).astype(BF16)
    merged, _ = merge(0)
    fsend[:, 0] = merged.T.reshape(NX * NU, TOK, HD).astype(BF16)

    for i in range(1, NX * NU):
        px, pu = plane(i)
        copy = remote(fsend.at[px * NU + pu], frecv.at[me], fs.at[i], fr.at[me], px, z, pu)
        copy.start()
        sends.append(copy)
    pltpu.make_async_copy(fsend.at[me], frecv.at[me], fr.at[me]).start()
    landed(lambda i: frecv.at[i], fr)
    for uu in range(NU):
        for half in range(2):
            ends = (frecv.at[2 * half * NU + uu], frecv.at[(2 * half + 1) * NU + uu])
            head = HEADS * uu + 3 * half
            out_ref[head] = ends[0][0]
            out_ref[head + 2] = ends[1][0]
            levels = []
            for end in ends:
                tail = end[2].astype(F32)
                levels.append(tail[:, 0:1] + tail[:, 1:2] + tail[:, 2:3])
            top = jnp.maximum(levels[0], levels[1])
            w = [jnp.exp2(level - top) for level in levels]
            both = [end[1].astype(F32) for end in ends]
            mixed = (both[0] * w[0] + both[1] * w[1]) / (w[0] + w[1])
            out_ref[head + 1] = mixed.astype(BF16)

    for copy in sends:
        copy.wait_send()
    to_plane(lambda copy: copy.wait_send(), (2, 1, 3, 0), 0)
    to_plane(lambda copy: copy.wait_send(), (2, 1, 3), 1)
    for k in range(1, NZ):
        pltpu.make_async_copy(osend.at[k], osend.at[k], os.at[k]).wait()


def shards(queries, keys_new, values_new, keys_cache, values_cache, query_frame, context_frame):
    hbm = pl.BlockSpec(memory_space=pltpu.HBM)
    vmem = pl.BlockSpec(memory_space=pltpu.VMEM)
    dma = pltpu.SemaphoreType.DMA
    n = NX * NU

    def by_head(rows):
        return rows.reshape(TOK, NU * HEADS, HD).transpose(1, 0, 2)

    out = pl.pallas_call(
        kernel,
        out_shape=jax.ShapeDtypeStruct((NU * HEADS, TOK, HD), BF16),
        in_specs=[hbm] * 7,
        out_specs=vmem,
        scratch_shapes=[
            pltpu.VMEM((8, 128), jnp.int32),
            pltpu.VMEM((56, 128), jnp.int32),
            pltpu.VMEM((3, NU * HEADS, TOK, HD), BF16),
            pltpu.VMEM((HEADS, 2, CTXB, HD), BF16),
            pltpu.VMEM((2, n, TOK, HD), BF16),
            pltpu.VMEM((2, 2, n, TOK, HD), BF16),
            pltpu.VMEM((NZ, n, TOK, HD), BF16),
            pltpu.VMEM((2 * NX, 2, KB, HD), BF16),
            pltpu.VMEM((2 * NX, HD, KB), BF16),
            pltpu.VMEM((2 * NX, KB, 128), F32),
            pltpu.VMEM((2 * NX, KB, 128), jnp.int32),
            pltpu.VMEM((NZ, 8, 128), jnp.int32),
            pltpu.VMEM((NZ, HD + 16, 128), BF16),
            pltpu.VMEM((NZ, HD + 16, 128), BF16),
            pltpu.VMEM((n, 3, TOK, HD), BF16),
            pltpu.VMEM((n, 3, TOK, HD), BF16),
            dma((3,)), dma((HEADS, 2)), dma((2,)),
            dma((n,)), dma((n,)),
            dma((2, n)), dma((2, n)),
            dma((NZ,)), dma((NZ,)),
            dma((2 * NX,)), dma((2 * NX,)),
            dma((NZ,)), dma((NZ,)),
            dma((n,)), dma((n,)),
        ],
        compiler_params=pltpu.CompilerParams(
            collective_id=0, has_side_effects=True, vmem_limit_bytes=64 * 2**20
        ),
    )(
        by_head(queries), by_head(keys_new), by_head(values_new), keys_cache, values_cache,
        query_frame.reshape(8, 128), context_frame.reshape(56, 128),
    )
    return out.transpose(1, 0, 2).reshape(queries.shape)


def solution(mesh):
    return jax.shard_map(
        shards,
        mesh=mesh,
        in_specs=(
            P(("rep", "blk", "uly"), None),
            P(("rep", "blk", "uly"), None),
            P(("rep", "blk", "uly"), None),
            P(("rep", "blk"), "uly"),
            P(("rep", "blk"), "uly"),
            P("rep"),
            P("rep"),
        ),
        out_specs=P(("rep", "blk", "uly"), None),
        check_vma=False,
    )
```

```python
import functools
import math

import jax
import jax.numpy as jnp
from jax import lax
from jax.experimental import pallas as pl
from jax.experimental.pallas import tpu as pltpu
from jax.sharding import PartitionSpec as P

HD = 128
NX, NZ, NU = 4, 8, 4
TOK = 8
CTXB = 224
NEWB = NU * TOK
KB = CTXB + NEWB
HEADS = 6
SCALE = math.log2(math.e) / math.sqrt(HD)
LOW = -1e30
MESH = pl.DeviceIdType.MESH
F32, BF16 = jnp.float32, jnp.bfloat16


def pair_start(x):
    return 3 * (x // 2) + lax.rem(x, 2)


def kernel(
    q_ref, kn_ref, vn_ref, kc_ref, vc_ref, qf_hbm, cf_hbm, out_ref,
    qf_ref, cf_ref,    qstage, nstage, cache, qland, qz, nland, qall, kvbuf, vt, sbuf, kft, qfr, osend, orecv, fsend, frecv,
    st, ct, fr_sem, qs, qr, ns, nr, zs, zr, ks, kr, os, orr, fs, fr,
):
    blk, u = lax.axis_index("blk"), lax.axis_index("uly")
    x, z = blk // NZ, lax.rem(blk, NZ)
    me = x * NU + u
    slot = lax.rem(z, 2)
    other = z + 1 - 2 * slot
    base = z - slot
    even = lax.rem(x + z, 2) == 0
    role = lax.rem(x + z, 2)

    def at(x_, z_, u_):
        return {"blk": x_ * NZ + z_, "uly": u_}

    def plane(i):
        dx, du = i // NU, i % NU
        return lax.rem(x + dx, NX), lax.rem(u + du, NU)

    def along(k):
        return at(x, lax.rem(z + NZ - k, NZ), u)

    staged = [
        pltpu.make_async_copy(q_ref, qstage, st.at[0]),
        pltpu.make_async_copy(kn_ref, nstage.at[:, 0], st.at[1]),
        pltpu.make_async_copy(vn_ref, nstage.at[:, 1], st.at[2]),
    ]
    frame_copies = [
        pltpu.make_async_copy(qf_hbm, qf_ref, fr_sem.at[0]),
        pltpu.make_async_copy(cf_hbm, cf_ref, fr_sem.at[1]),
    ]
    cache_copies = [
        pltpu.make_async_copy(ref.at[:, pl.ds(h * HD, HD)], cache.at[h, i], ct.at[h, i])
        for h in range(HEADS)
        for i, ref in enumerate((kc_ref, vc_ref))
    ]
    for copy in staged + cache_copies + frame_copies:
        copy.start()

    barrier = pltpu.get_barrier_semaphore()
    for i in range(1, NX * NU):
        px, pu = plane(i)
        pl.semaphore_signal(barrier, inc=1, device_id=at(px, z, pu), device_id_type=MESH)
    for k in range(1, NZ):
        pl.semaphore_signal(barrier, inc=1, device_id=along(k), device_id_type=MESH)
    for i in range(1, NX * NU):
        px, pu = plane(i)
        pl.semaphore_signal(barrier, inc=1, device_id=at(px, other, pu), device_id_type=MESH)
    for copy in frame_copies:
        copy.wait()
    lanes = lax.broadcasted_iota(jnp.int32, (1, 128), 1)
    for zz in range(NZ):
        row = jnp.zeros((1, 128), jnp.int32)
        for xx in range(NX):
            part = qf_ref[pl.ds(2 * xx + zz // 4, 1), :]
            part = pltpu.roll(part, (xx * 32 - (zz % 4) * 32) % 128, 1)
            row = jnp.where(lanes // 32 == xx, part, row)
        qfr[zz] = jnp.broadcast_to(row, (8, 128))
    for block in range(2 * NX):
        xx, bz = block % NX, base + block // NX
        place = (xx * NZ + bz) * CTXB
        first, off = place // 128, lax.rem(place, 128)
        rows = [
            pltpu.roll(
                jnp.broadcast_to(cf_ref[pl.ds(jnp.minimum(first + j, 55), 1), :], (8, 128)),
                lax.rem(128 - off, 128),
                1,
            )
            for j in range(3)
        ]
        lanes8 = lax.broadcasted_iota(jnp.int32, (8, 128), 1)
        low = jnp.where(lanes8 < 128 - off, rows[0], rows[1])
        high = jnp.where(lanes8 < 128 - off, rows[1], rows[2])
        token = (xx * NZ + bz) * NEWB
        new = jnp.broadcast_to(qf_ref[pl.ds(token // 128, 1), :], (8, 128))
        new = pltpu.roll(new, lax.rem(96 + 128 - lax.rem(token, 128), 128), 1)
        high = jnp.where(lanes8 >= 96, new, high)
        for h, part in enumerate((low, high)):
            wide = jnp.broadcast_to(part[:1].astype(F32), (128, 128))
            kft[block, pl.ds(h * 128, 128), :] = wide.T.astype(jnp.int32)

    pl.semaphore_wait(barrier, 2 * (NX * NU - 1) + NZ - 1)
    for copy in staged:
        copy.wait()

    def remote(src, dst, ssem, rsem, px, pz, pu):
        return pltpu.make_async_remote_copy(
            src_ref=src,
            dst_ref=dst,
            send_sem=ssem,
            recv_sem=rsem,
            device_id=at(px, pz, pu),
            device_id_type=MESH,
        )

    def heads(px, pu):
        return HEADS * pu + pair_start(px)

    sends = []
    for i in range(1, NX * NU):
        px, pu = plane(i)
        src = qstage.at[pl.ds(heads(px, pu), 2)]
        sends.append(remote(src, qland.at[me], qs.at[i], qr.at[me], px, z, pu))
    for n, pz in enumerate((z, other)):
        for i in range(1 - n, NX * NU):
            px, pu = plane(i)
            src = nstage.at[heads(px, pu) + lax.rem(pz, 2)]
            dst = nland.at[slot, me]
            sends.append(remote(src, dst, ns.at[n, i], nr.at[slot, me], px, pz, pu))
    def go(copies):
        for copy in copies:
            copy.start()

    n = NX * NU
    group, new_here, new_other = sends[: n - 1], sends[n - 1 : 2 * n - 2], sends[2 * n - 2 :]
    go(group)
    go(new_other)
    pltpu.make_async_copy(qstage.at[pl.ds(heads(x, u), 2)], qland.at[me], qr.at[me]).start()
    pltpu.make_async_copy(
        nstage.at[heads(x, u) + slot], nland.at[slot, me], nr.at[slot, me]
    ).start()

    def landed(dst, rsem, count=NX * NU):
        for i in range(count):
            pltpu.make_async_copy(dst(i), dst(i), rsem.at[i]).wait()

    def cached(px, pz, ssem):
        whole = lax.rem(px + pz, 2) == 0
        dst = jnp.where(whole, slot * NX + x, x)
        return remote(
            cache.at[pair_start(px) + lax.rem(pz, 2)],
            kvbuf.at[dst, :, pl.ds(0, CTXB)],
            ks.at[ssem],
            kr.at[dst],
            px,
            pz,
            u,
        )

    def takes(px, pz):
        return (lax.rem(px + pz, 2) == 0) | (pz == z)

    def to_plane(act, steps, n):
        for step in steps:
            px, pz = lax.rem(x + step, NX), (other, z)[n]

            @pl.when(takes(px, pz))
            def _():
                act(cached(px, pz, 2 * step + n))

    for copy in cache_copies:
        copy.wait()
    to_plane(lambda copy: copy.start(), (2, 1, 3, 0), 0)
    go(new_here)
    own_slot = jnp.where(even, slot * NX + x, x)
    pltpu.make_async_copy(
        cache.at[pair_start(x) + slot], kvbuf.at[own_slot, :, pl.ds(0, CTXB)], kr.at[own_slot]
    ).start()

    landed(lambda i: qland.at[i], qr)
    for h in range(2):
        qz[h] = qland[:, h]
    for k in (4, 3, 5, 2, 6, 1, 7):
        pz = lax.rem(z + k, NZ)
        copy = remote(qz.at[lax.rem(pz, 2)], qall.at[k], zs.at[k], zr.at[k], x, pz, u)
        copy.start()
        sends.append(copy)
    to_plane(lambda copy: copy.start(), (2, 1, 3), 1)
    qall[0] = qz[slot]

    for p in range(2):
        landed(lambda i: nland.at[p, i], nr.at[p])

    def join(dst, xx, p):
        rows = kvbuf.at[dst, :, pl.ds(0, CTXB)]
        pltpu.make_async_copy(rows, rows, kr.at[dst]).wait()
        for i in range(2):
            new = nland[p, pl.ds(xx * NU, NU), i].astype(F32).reshape(NEWB, HD)
            kvbuf[dst, i, pl.ds(CTXB, NEWB), :] = new.astype(BF16)
        vt[dst] = kvbuf[dst, 1].T

    def order(i):
        odd = lax.rem(i, 2)
        return odd * lax.rem(4 + (i + 1) // 2, NZ) + (1 - odd) * (4 - i // 2)

    def attend(blocks, i):
        k = order(i)

        @pl.when(k > 0)
        def _():
            pltpu.make_async_copy(qall.at[k], qall.at[k], zr.at[k]).wait()

        zz = lax.rem(z + NZ - k, NZ)
        query = qall[k].astype(F32).reshape(NX * NU * TOK, HD).astype(BF16)
        frames = qfr[zz][:1]
        top = jnp.full((8, 128), LOW, F32)
        for dst, block in blocks:
            s = lax.dot_general(
                kvbuf[dst, 0], query, (((1,), (1,)), ((), ())), preferred_element_type=F32
            )
            s = jnp.where(kft[block] <= frames, s * SCALE, LOW)
            sbuf[dst] = s
            top = jnp.maximum(top, jnp.max(s.reshape(KB // 8, 8, 128), axis=0))
        top = jnp.max(top, axis=0, keepdims=True)
        total = jnp.zeros((8, 128), F32)
        summed = jnp.zeros((HD, 128), F32)
        for dst, _ in blocks:
            w = jnp.exp2(sbuf[dst] - top)
            total += jnp.sum(w.reshape(KB // 8, 8, 128), axis=0)
            summed += jnp.dot(vt[dst], w.astype(BF16), preferred_element_type=F32)
        total = jnp.sum(total, axis=0, keepdims=True)
        osend[k, pl.ds(0, HD), :] = (summed / total).astype(BF16)
        level = top + jnp.log2(total)
        one = level.astype(BF16).astype(F32)
        two = (level - one).astype(BF16).astype(F32)
        three = level - one - two
        row = lax.broadcasted_iota(jnp.int32, (16, 128), 0)
        rows = jnp.where(row == 0, one, jnp.where(row == 1, two, jnp.where(row == 2, three, 0.0)))
        osend[k, pl.ds(HD, 16), :] = rows.astype(BF16)

        @pl.when(k > 0)
        def _():
            pltpu.make_async_remote_copy(
                src_ref=osend.at[k],
                dst_ref=orecv.at[k],
                send_sem=os.at[k],
                recv_sem=orr.at[k],
                device_id=along(k),
                device_id_type=MESH,
            ).start()

    def work(blocks):
        for dst, block in blocks:
            xx = lax.rem(block, NX)
            join(dst, xx, block // NX)

        def chunk(i, carry):
            attend(blocks, i)
            return carry

        lax.fori_loop(0, NZ, chunk, 0)

    @pl.when(even)
    def _():
        work([(b, b) for b in range(2 * NX)])

    @pl.when(jnp.logical_not(even))
    def _():
        work([(b, slot * NX + b) for b in range(NX)])

    orecv[0] = osend[0]

    for k in range(1, NZ):
        pltpu.make_async_copy(orecv.at[k], orecv.at[k], orr.at[k]).wait()

    def merge(kind):
        parity = lax.rem(role + kind, 2)
        parts = [orecv.at[2 * j + parity] for j in range(NZ // 2)]
        levels = []
        for part in parts:
            tail = part[pl.ds(HD, 16), :].astype(F32)
            levels.append(tail[0:1] + tail[1:2] + tail[2:3])
        top = functools.reduce(jnp.maximum, levels)
        weights = [jnp.exp2(level - top) for level in levels]
        total = functools.reduce(jnp.add, weights)
        merged = jnp.zeros((HD, 128), F32)
        for part, w in zip(parts, weights):
            merged += part[pl.ds(0, HD), :].astype(F32) * w
        return merged / total, top + jnp.log2(total)

    merged, level = merge(1)
    fsend[:, 1] = merged.T.reshape(NX * NU, TOK, HD).astype(BF16)
    one = level.astype(BF16).astype(F32)
    two = (level - one).astype(BF16).astype(F32)
    three = level - one - two
    row = lax.broadcasted_iota(jnp.int32, (128, 128), 0)
    level = jnp.where(row == 0, one, jnp.where(row == 1, two, jnp.where(row == 2, three, 0.0)))
    fsend[:, 2] = level.T.reshape(NX * NU, TOK, HD).astype(BF16)
    merged, _ = merge(0)
    fsend[:, 0] = merged.T.reshape(NX * NU, TOK, HD).astype(BF16)

    for i in range(1, NX * NU):
        px, pu = plane(i)
        copy = remote(fsend.at[px * NU + pu], frecv.at[me], fs.at[i], fr.at[me], px, z, pu)
        copy.start()
        sends.append(copy)
    pltpu.make_async_copy(fsend.at[me], frecv.at[me], fr.at[me]).start()
    landed(lambda i: frecv.at[i], fr)
    for uu in range(NU):
        for half in range(2):
            ends = (frecv.at[2 * half * NU + uu], frecv.at[(2 * half + 1) * NU + uu])
            head = HEADS * uu + 3 * half
            out_ref[head] = ends[0][0]
            out_ref[head + 2] = ends[1][0]
            levels = []
            for end in ends:
                tail = end[2].astype(F32)
                levels.append(tail[:, 0:1] + tail[:, 1:2] + tail[:, 2:3])
            top = jnp.maximum(levels[0], levels[1])
            w = [jnp.exp2(level - top) for level in levels]
            both = [end[1].astype(F32) for end in ends]
            mixed = (both[0] * w[0] + both[1] * w[1]) / (w[0] + w[1])
            out_ref[head + 1] = mixed.astype(BF16)

    for copy in sends:
        copy.wait_send()
    to_plane(lambda copy: copy.wait_send(), (2, 1, 3, 0), 0)
    to_plane(lambda copy: copy.wait_send(), (2, 1, 3), 1)
    for k in range(1, NZ):
        pltpu.make_async_copy(osend.at[k], osend.at[k], os.at[k]).wait()


def shards(queries, keys_new, values_new, keys_cache, values_cache, query_frame, context_frame):
    hbm = pl.BlockSpec(memory_space=pltpu.HBM)
    vmem = pl.BlockSpec(memory_space=pltpu.VMEM)
    dma = pltpu.SemaphoreType.DMA
    n = NX * NU

    def by_head(rows):
        return rows.reshape(TOK, NU * HEADS, HD).transpose(1, 0, 2)

    out = pl.pallas_call(
        kernel,
        out_shape=jax.ShapeDtypeStruct((NU * HEADS, TOK, HD), BF16),
        in_specs=[hbm] * 7,
        out_specs=vmem,
        scratch_shapes=[
            pltpu.VMEM((8, 128), jnp.int32),
            pltpu.VMEM((56, 128), jnp.int32),
            pltpu.VMEM((NU * HEADS, TOK, HD), BF16),
            pltpu.VMEM((NU * HEADS, 2, TOK, HD), BF16),
            pltpu.VMEM((HEADS, 2, CTXB, HD), BF16),
            pltpu.VMEM((n, 2, TOK, HD), BF16),
            pltpu.VMEM((2, n, TOK, HD), BF16),
            pltpu.VMEM((2, n, 2, TOK, HD), BF16),
            pltpu.VMEM((NZ, n, TOK, HD), BF16),
            pltpu.VMEM((2 * NX, 2, KB, HD), BF16),
            pltpu.VMEM((2 * NX, HD, KB), BF16),
            pltpu.VMEM((2 * NX, KB, 128), F32),
            pltpu.VMEM((2 * NX, KB, 128), jnp.int32),
            pltpu.VMEM((NZ, 8, 128), jnp.int32),
            pltpu.VMEM((NZ, HD + 16, 128), BF16),
            pltpu.VMEM((NZ, HD + 16, 128), BF16),
            pltpu.VMEM((n, 3, TOK, HD), BF16),
            pltpu.VMEM((n, 3, TOK, HD), BF16),
            dma((3,)), dma((HEADS, 2)), dma((2,)),
            dma((n,)), dma((n,)),
            dma((2, n)), dma((2, n)),
            dma((NZ,)), dma((NZ,)),
            dma((2 * NX,)), dma((2 * NX,)),
            dma((NZ,)), dma((NZ,)),
            dma((n,)), dma((n,)),
        ],
        compiler_params=pltpu.CompilerParams(
            collective_id=0, has_side_effects=True, vmem_limit_bytes=64 * 2**20
        ),
    )(
        by_head(queries), by_head(keys_new), by_head(values_new), keys_cache, values_cache,
        query_frame.reshape(8, 128), context_frame.reshape(56, 128),
    )
    return out.transpose(1, 0, 2).reshape(queries.shape)


def solution(mesh):
    return jax.shard_map(
        shards,
        mesh=mesh,
        in_specs=(
            P(("rep", "blk", "uly"), None),
            P(("rep", "blk", "uly"), None),
            P(("rep", "blk", "uly"), None),
            P(("rep", "blk"), "uly"),
            P(("rep", "blk"), "uly"),
            P("rep"),
            P("rep"),
        ),
        out_specs=P(("rep", "blk", "uly"), None),
        check_vma=False,
    )
```
